256 devices in a mesh: row: 8 (over z), col: 16 (over y, x), layer: 2 (over core).
Axes of the slice: x: 4, y: 4, z: 8, core: 2. Of those that a mesh axis runs over, the one named last changes fastest.
Arguments:
- amplitudes: bfloat16 [4096, 12288], P('row', ('col', 'layer')), may hold values from -6 to 6
- integrals: bfloat16 [12288, 12288], P(('col', 'layer')), may hold values from -0.109375 to 0.109375
- hole_integrals: bfloat16 [4096, 4096], P('row'), may hold values from -0.09375 to 0.09375
- tile_mask: int32 [96, 96], replicated, may hold values 0 or 1
- occupied_energy: float32 [4096], P('row'), may hold values from -3 to -0.5
- virtual_energy: float32 [12288], P(('col', 'layer')), may hold values from 0.5 to 4
Outputs:
- update: float32 [4096, 12288], P('row', ('col', 'layer'))
The draws below stay inside these ranges and needn't reach their ends.
All inputs are finite; a program needn't handle non-finite values.
Results may differ from the reference program's by a relative error of at most 0.0003.
Values may be sent and summed in bfloat16 or wider, within the bound.
No kernel may reach another device: no remote copies, remote signals or barrier semaphores. Data moves between devices by JAX's collectives and lax.ppermute only.
A program may use at most 128 MiB of HBM per device.

```python
import jax
import jax.numpy as jnp

TB = 128
OCC = 4096
VP = 12288
TILES = 96


def touch_ends(result, stream_key, smallest, high):
    index_at = [jax.random.randint(jax.random.fold_in(stream_key, axis), (), 0, length) for axis, length in enumerate(result.shape)]
    main_axis = result.shape.index(max(result.shape))
    next_to = index_at[:main_axis] + [(index_at[main_axis] + 1) % result.shape[main_axis]] + index_at[main_axis + 1:]
    return result.at[tuple(index_at)].set(smallest).at[tuple(next_to)].set(high)


def raised(result, rng, source, target, shards_of, factor):
    owner, partner = [(jnp.arange(result.shape[axis_at]) // (result.shape[axis_at] // shards_of)).reshape([-1 if axis == axis_at else 1 for axis in range(result.ndim)]) for axis_at in (source, target)]
    chosen = jax.random.permutation(rng, shards_of)[partner]
    strong = (owner == chosen) | (owner == (partner + shards_of // 2) % shards_of)
    return jnp.where(strong, factor * result, result)


def steps_of(own_key, dims, pieces, low, high):
    gain, own = 1.0, jax.random.fold_in(own_key, 6)
    for axis_at, blocks in pieces:
        heights = jnp.exp(jax.random.uniform(jax.random.fold_in(own, axis_at), (blocks,), jnp.float32, low / len(pieces), high / len(pieces)))
        gain = gain * jnp.repeat(heights, dims[axis_at] // blocks).reshape([-1 if axis == axis_at else 1 for axis in range(len(dims))])
    return gain


def scatter_about(key, shape, width, bound, pieces=(), held_as=jnp.bfloat16):
    drawn = jax.random.normal(key, shape, jnp.float32) * width
    if len(pieces) > 0:
        drawn = steps_of(key, shape, pieces, -0.22, 0.18) * drawn
    return jnp.clip(drawn, min=-bound, max=bound).astype(held_as)


def bell_draw_with(own_key, extent, spread, reach, cuts, heavy, kind=jnp.bfloat16):
    values = spread * jax.random.normal(own_key, extent, jnp.float32)
    if cuts:
        values = values * steps_of(own_key, extent, cuts, -0.22, 0.18)
    return jnp.clip(raised(values, jax.random.fold_in(own_key, 3), *heavy), -reach, reach).astype(kind)


def setup_inputs(seed: int = 0) -> dict:
    keys = jax.random.split(jax.random.key(seed), 7)
    amplitudes = scatter_about(keys[0], (OCC, VP), 1.0, 6.0, ((0, 8), (1, 32)))
    integrals = bell_draw_with(keys[1], (VP, VP), VP ** -0.5, 0.109375, ((0, 32),), (0, 1, 32, 2.75))
    hole_integrals = scatter_about(keys[2], (OCC, OCC), OCC ** -0.5, 0.09375, ((0, 8),))
    tile_mask = touch_ends((jax.random.randint(keys[3], (TILES, TILES), 0, 4) < 3).astype(jnp.int32), jax.random.fold_in(keys[3], 1), 0, 1)
    occupied_energy = jnp.clip(-3.0 + 2.5 * jax.random.uniform(keys[4], (OCC,), jnp.float32) ** steps_of(keys[4], (OCC,), ((0, 8),), -0.2, 0.2), -3.0, -0.5)
    virtual_energy = jnp.clip(0.5 + 3.5 * jax.random.uniform(keys[5], (VP,), jnp.float32) ** steps_of(keys[5], (VP,), ((0, 32),), -0.2, 0.2), 0.5, 4.0)
    return {"amplitudes": amplitudes, "integrals": integrals, "hole_integrals": hole_integrals, "tile_mask": tile_mask, "occupied_energy": occupied_energy, "virtual_energy": virtual_energy}


def reference(amplitudes, integrals, hole_integrals, tile_mask, occupied_energy, virtual_energy):
    expanded = jnp.repeat(jnp.repeat(tile_mask, TB, axis=0), TB, axis=1).astype(jnp.bfloat16)
    masked = integrals * expanded
    ladder = jnp.dot(amplitudes, masked, preferred_element_type=jnp.float32)
    holes = jnp.dot(hole_integrals, amplitudes, preferred_element_type=jnp.float32)
    denominator = virtual_energy[None, :] - occupied_energy[:, None]
    return (ladder + holes) / denominator
```

```python
import functools

import jax
import jax.numpy as jnp
from jax import lax
from jax.experimental import pallas as pl
from jax.experimental.pallas import tpu as pltpu
from jax.sharding import PartitionSpec as P

TB = 128
X = 4
Y = 4
F32 = jnp.float32
I16 = jnp.int16
I32 = jnp.int32
BF16 = jnp.bfloat16
TOP = 32700.0
STEPS = 64.0
VMEM = 48 * 1024 * 1024


def shift_x(d):
    return [(y * X + x, y * X + (x + d) % X) for y in range(Y) for x in range(X)]


def shift_y(d):
    return [(y * X + x, ((y + d) % Y) * X + x) for y in range(Y) for x in range(X)]


def encode(block):
    peak = jnp.maximum(jnp.max(jnp.abs(block), axis=0, keepdims=True), 1e-30)
    code = jnp.floor(jnp.log2(TOP / peak) * STEPS)
    scale = jnp.exp2(code * (1.0 / STEPS))
    return jnp.round(block * scale).astype(I32).astype(I16), code


def decode(block, code):
    scale = jnp.exp2(code.astype(F32) * (1.0 / STEPS))
    return block.astype(I32).astype(F32) * (1.0 / scale)


def put_code(ref, start, row, code):
    rows = ref[pl.ds(start, 16), :].astype(I32)
    at = lax.broadcasted_iota(I32, rows.shape, 0) == row
    ref[pl.ds(start, 16), :] = jnp.where(at, code.astype(I32), rows).astype(I16)


def get_code(ref, start, row):
    rows = ref[pl.ds(start, 16), :].astype(I32)
    at = lax.broadcasted_iota(I32, rows.shape, 0) == row
    return jnp.sum(jnp.where(at, rows, 0).astype(F32), axis=0, keepdims=True)


def pick(i, table):
    out = jnp.int32(table[-1])
    for k in range(len(table) - 2, -1, -1):
        out = jnp.where(i == k, jnp.int32(table[k]), out)
    return out


def column_block(meta, dx, dy, other_layer):
    x = lax.rem(meta[0] + dx, X)
    y = lax.rem(meta[1] + dy, Y)
    layer = 1 - meta[2] if other_layer else meta[2]
    return (y * X + x) * 2 + layer


def masked(meta, tiles, block_at, v_ref):
    rows = []
    for kt in range(tiles):
        row = []
        for qt in range(tiles):
            m = meta[3 + kt * 96 + block_at * tiles + qt].astype(F32)
            keep = jnp.broadcast_to(m, (TB, TB)).astype(BF16)
            row.append(v_ref[kt * TB:(kt + 1) * TB, qt * TB:(qt + 1) * TB] * keep)
        rows.append(jnp.concatenate(row, axis=1))
    return jnp.concatenate(rows, axis=0)


def params():
    return pltpu.CompilerParams(vmem_limit_bytes=VMEM)


def cost(flops, moved):
    return pl.CostEstimate(flops=flops, bytes_accessed=moved, transcendentals=0)


FIRST = [(2, 0), (2, 1), (2, 2), (2, 3), (0, 2), (1, 2), (3, 2)]
SECOND = [(dx, dy) for dx in (0, 1, 3) for dy in (0, 1, 3)]


def pack(meta, integrals, width, dests):
    n = len(dests)

    def body(meta_ref, v_ref, out_ref):
        i = pl.program_id(0)
        at = column_block(meta_ref, pick(i, [d[0] for d in dests]), pick(i, [d[1] for d in dests]), True)
        out_ref[0] = masked(meta_ref, width // TB, at, v_ref)

    def v_map(i, meta_ref):
        return 0, column_block(meta_ref, pick(i, [d[0] for d in dests]), pick(i, [d[1] for d in dests]), True)

    return pl.pallas_call(
        body,
        out_shape=jax.ShapeDtypeStruct((n, width, width), BF16),
        grid_spec=pltpu.PrefetchScalarGridSpec(
            num_scalar_prefetch=1,
            grid=(n,),
            in_specs=[pl.BlockSpec((width, width), v_map)],
            out_specs=pl.BlockSpec((1, width, width), lambda i, m: (i, 0, 0)),
        ),
        compiler_params=params(),
        cost_estimate=cost(0, 4 * n * width * width),
        name="pack",
    )(meta, integrals)


def dest(axis, d, o):
    return (d, o) if axis == 0 else (o, d)


def product(meta_ref, at, width, v_ref, vp, a_s, v_s):
    v_s[:width, :] = masked(meta_ref, width // TB, at, v_ref)
    v_s[width:, :] = vp
    return jnp.dot(a_s[...], v_s[...], preferred_element_type=F32)


def load_a(a_ref, ap_ref, a_s, width):
    @pl.when(pl.program_id(0) == 0)
    def _():
        a_s[:, :width] = a_ref[...]
        a_s[:, width:] = ap_ref[...]


def far(axis, meta, a, ap, integrals, v1):
    rows, width = a.shape
    half, q = rows // 2, rows // 4
    table = [FIRST.index(dest(axis, 2, o)) for o in range(4)]
    msg = 4 * q + 16

    def place(i):
        return (2, i) if axis == 0 else (i, 2)

    def body(meta_ref, a_ref, ap_ref, v_ref, vp_ref, up_ref, down_ref, a_s, v_s):
        i = pl.program_id(0)
        load_a(a_ref, ap_ref, a_s, width)
        at = column_block(meta_ref, *place(i), False)
        part = product(meta_ref, at, width, v_ref, vp_ref[0], a_s, v_s)
        for ref, lo in ((up_ref, 0), (down_ref, q)):
            coded, code = encode(part[lo:lo + q])
            ref[pl.ds(pl.multiple_of(i * q, q), q), :] = coded
            put_code(ref, 4 * q, i, code)

    return pl.pallas_call(
        body,
        out_shape=[jax.ShapeDtypeStruct((msg, width), I16)] * 2,
        grid_spec=pltpu.PrefetchScalarGridSpec(
            num_scalar_prefetch=1,
            grid=(4,),
            in_specs=[
                pl.BlockSpec((half, width), lambda i, m: (axis, 0)),
                pl.BlockSpec((half, width), lambda i, m: (axis, 0)),
                pl.BlockSpec((width, width), lambda i, m: (0, column_block(m, *place(i), False))),
                pl.BlockSpec((1, width, width), lambda i, m: (pick(i, table), 0, 0)),
            ],
            out_specs=[pl.BlockSpec((msg, width), lambda i, m: (0, 0))] * 2,
            scratch_shapes=[pltpu.VMEM((half, 2 * width), BF16), pltpu.VMEM((2 * width, width), BF16)],
        ),
        compiler_params=params(),
        cost_estimate=cost(2 * 4 * half * 2 * width * width, 4 * 4 * width * width),
        name="far_y" if axis else "far_x",
    )(meta, a, ap, integrals, v1)


NEAR = [(1, 2), (3, 2), (1, 0), (1, 1), (1, 3), (3, 0), (3, 1), (3, 3)]
HOME = [(0, 2), (0, 0), (0, 1), (0, 3)]


def v_tables(axis, steps):
    one, two = [], []
    for d, o in steps:
        at = dest(axis, d, o)
        one.append(FIRST.index(at) if at in FIRST else None)
        two.append(SECOND.index(at) if at in SECOND else None)
    for t in (one, two):
        known = [v for v in t if v is not None]
        last = known[0]
        for k, v in enumerate(t):
            last = v if v is not None else last
            t[k] = last
    return one, two


def near(axis, meta, a, ap, integrals, v1, v2):
    rows, width = a.shape
    half, q = rows // 2, rows // 4
    msg = 4 * q + 16
    one, two = v_tables(axis, NEAR)

    def spot(i):
        return pick(i, [s[0] for s in NEAR]), pick(i, [s[1] for s in NEAR])

    def body(meta_ref, a_ref, ap_ref, v_ref, v1_ref, v2_ref, up_ref, down_ref, up_st, down_st, a_s, v_s):
        i = pl.program_id(0)
        load_a(a_ref, ap_ref, a_s, width)
        d, o = spot(i)
        at = column_block(meta_ref, *dest(axis, d, o), False)
        vp = jnp.where(i < 2, v1_ref[0], v2_ref[0])
        part = product(meta_ref, at, width, v_ref, vp, a_s, v_s)
        here = pl.ds(pl.multiple_of(o * q, q), q)

        @pl.when(d == 1)
        def _():
            up_st[here, :] = part[:q]
            coded, code = encode(part[q:])
            up_ref[here, :] = coded
            put_code(up_ref, 4 * q, o, code)

        @pl.when(d == 3)
        def _():
            down_st[here, :] = part[q:]
            coded, code = encode(part[:q])
            down_ref[here, :] = coded
            put_code(down_ref, 4 * q, o, code)

    whole = lambda n: pl.BlockSpec((n, width), lambda i, m: (0, 0))
    return pl.pallas_call(
        body,
        out_shape=[jax.ShapeDtypeStruct((msg, width), I16)] * 2 + [jax.ShapeDtypeStruct((4 * q, width), F32)] * 2,
        grid_spec=pltpu.PrefetchScalarGridSpec(
            num_scalar_prefetch=1,
            grid=(len(NEAR),),
            in_specs=[
                pl.BlockSpec((half, width), lambda i, m: (axis, 0)),
                pl.BlockSpec((half, width), lambda i, m: (axis, 0)),
                pl.BlockSpec((width, width), lambda i, m: (0, column_block(m, *dest(axis, *spot(i)), False))),
                pl.BlockSpec((1, width, width), lambda i, m: (pick(i, one), 0, 0)),
                pl.BlockSpec((1, width, width), lambda i, m: (pick(i, two), 0, 0)),
            ],
            out_specs=[whole(msg), whole(msg), whole(4 * q), whole(4 * q)],
            scratch_shapes=[pltpu.VMEM((half, 2 * width), BF16), pltpu.VMEM((2 * width, width), BF16)],
        ),
        compiler_params=params(),
        cost_estimate=cost(2 * 8 * half * 2 * width * width, 8 * 4 * width * width),
        name="near_y" if axis else "near_x",
    )(meta, a, ap, integrals, v1, v2)


def home(axis, meta, a, ap, integrals, v1, v2):
    rows, width = a.shape
    half = rows // 2
    one, two = v_tables(axis, HOME)

    def spot(i):
        return 0, pick(i, [s[1] for s in HOME])

    def body(meta_ref, a_ref, ap_ref, v_ref, v1_ref, v2_ref, out_ref, a_s, v_s):
        i = pl.program_id(0)
        load_a(a_ref, ap_ref, a_s, width)
        at = column_block(meta_ref, *dest(axis, *spot(i)), False)
        vp = jnp.where(i < 1, v1_ref[0], v2_ref[0])
        out_ref[0] = product(meta_ref, at, width, v_ref, vp, a_s, v_s)

    return pl.pallas_call(
        body,
        out_shape=jax.ShapeDtypeStruct((4, half, width), F32),
        grid_spec=pltpu.PrefetchScalarGridSpec(
            num_scalar_prefetch=1,
            grid=(len(HOME),),
            in_specs=[
                pl.BlockSpec((half, width), lambda i, m: (axis, 0)),
                pl.BlockSpec((half, width), lambda i, m: (axis, 0)),
                pl.BlockSpec((width, width), lambda i, m: (0, column_block(m, *dest(axis, *spot(i)), False))),
                pl.BlockSpec((1, width, width), lambda i, m: (pick(i, one), 0, 0)),
                pl.BlockSpec((1, width, width), lambda i, m: (pick(i, two), 0, 0)),
            ],
            out_specs=pl.BlockSpec((1, half, width), lambda i, m: (spot(i)[1], 0, 0)),
            scratch_shapes=[pltpu.VMEM((half, 2 * width), BF16), pltpu.VMEM((2 * width, width), BF16)],
        ),
        compiler_params=params(),
        cost_estimate=cost(2 * 4 * half * 2 * width * width, 4 * 4 * width * width),
        name="home_y" if axis else "home_x",
    )(meta, a, ap, integrals, v1, v2)


def relay(name, up_in, down_in, up_st, down_st):
    msg, width = up_in.shape
    q = (msg - 16) // 4

    def body(ui_ref, uc_ref, di_ref, dc_ref, us_ref, ds_ref, up_ref, down_ref):
        i = pl.program_id(0)
        here = pl.ds(pl.multiple_of(i * q, q), q)
        for got, codes, own, out in ((ui_ref, uc_ref, us_ref, up_ref), (di_ref, dc_ref, ds_ref, down_ref)):
            total = own[...] + decode(got[...], get_code(codes, 0, i))
            coded, code = encode(total)
            out[here, :] = coded
            put_code(out, 4 * q, i, code)

    data = pl.BlockSpec((q, width), lambda i: (i, 0))
    codes = pl.BlockSpec((16, width), lambda i: (4 * q // 16, 0))
    return pl.pallas_call(
        body,
        out_shape=[jax.ShapeDtypeStruct((msg, width), I16)] * 2,
        grid=(4,),
        in_specs=[data, codes, data, codes, data, data],
        out_specs=[pl.BlockSpec((msg, width), lambda i: (0, 0))] * 2,
        compiler_params=params(),
        cost_estimate=cost(0, 16 * q * width * 4),
        name=name,
    )(up_in, up_in, down_in, down_in, up_st, down_st)


def turn(name, st, first_near, first_far, second_near, second_far):
    _, half, width = st.shape
    q = half // 2

    def body(st_ref, fn, fnc, ff, ffc, sn, snc, sf, sfc, own_ref, m1_ref, m2_ref, m3_ref):
        i = pl.program_id(0)
        top = st_ref[0, :q] + decode(fn[...], get_code(fnc, 0, i)) + decode(ff[...], get_code(ffc, 0, i))
        low = st_ref[0, q:] + decode(sn[...], get_code(snc, 0, i)) + decode(sf[...], get_code(sfc, 0, i))

        @pl.when(i == 0)
        def _():
            own_ref[:q] = top
            own_ref[q:] = low

        for k, ref in ((1, m1_ref), (2, m2_ref), (3, m3_ref)):
            @pl.when(i == k)
            def _():
                for n, part in ((0, top), (1, low)):
                    coded, code = encode(part)
                    ref[n * q:(n + 1) * q, :] = coded
                    put_code(ref, 2 * q, n, code)

    data = pl.BlockSpec((q, width), lambda i: (i, 0))
    codes = pl.BlockSpec((16, width), lambda i: (4 * q // 16, 0))
    whole = lambda n: pl.BlockSpec((n, width), lambda i: (0, 0))
    return pl.pallas_call(
        body,
        out_shape=[jax.ShapeDtypeStruct((half, width), F32)] + [jax.ShapeDtypeStruct((half + 16, width), I16)] * 3,
        grid=(4,),
        in_specs=[pl.BlockSpec((1, half, width), lambda i: (i, 0, 0))] + [data, codes] * 4,
        out_specs=[whole(half)] + [whole(half + 16)] * 3,
        compiler_params=params(),
        cost_estimate=cost(0, 4 * half * width * 10),
        name=name,
    )(st, *[r for m in (first_near, first_far, second_near, second_far) for r in (m, m)])


def finish(own_x, own_y, got_x, got_y, holes, occupied, virtual):
    half, width = own_x.shape
    q = half // 2

    def body(ox, oy, x1, x2, x3, y1, y2, y3, holes_ref, occ_ref, virt_ref, out_ref):
        for own, got, lo in ((ox, (x1, x2, x3), 0), (oy, (y1, y2, y3), half)):
            for n in range(2):
                total = own[n * q:(n + 1) * q]
                for ref in got:
                    total = total + decode(ref[n * q:(n + 1) * q, :], get_code(ref, 2 * q, n))
                here = slice(lo + n * q, lo + (n + 1) * q)
                total = total + holes_ref[here, :]
                out_ref[here, :] = total / (virt_ref[...] - occ_ref[here, :])

    return pl.pallas_call(
        body,
        out_shape=jax.ShapeDtypeStruct((2 * half, width), F32),
        compiler_params=params(),
        cost_estimate=cost(0, 2 * half * width * 12),
        name="finish",
    )(own_x, own_y, *got_x, *got_y, holes, occupied[:, None], virtual[None, :])


def shards(amplitudes, integrals, hole_integrals, tile_mask, occupied_energy, virtual_energy):
    width = amplitudes.shape[1]
    tiles = width // TB
    col, layer = lax.axis_index("col"), lax.axis_index("layer")
    mask_rows = lax.dynamic_slice_in_dim(tile_mask, (col * 2 + layer) * tiles, tiles, 0)
    meta = jnp.concatenate([jnp.stack([lax.rem(col, X), lax.div(col, X), layer]).astype(I32), mask_rows.reshape(-1)])
    swap = [(0, 1), (1, 0)]

    gathered = lax.all_gather(amplitudes, "row", axis=0, tiled=True)
    a, ap = amplitudes, lax.ppermute(amplitudes, "layer", swap)
    v1 = lax.ppermute(pack(meta, integrals, width, FIRST), "layer", swap)
    v2 = lax.ppermute(pack(meta, integrals, width, SECOND), "layer", swap)

    shift = (shift_x, shift_y)
    send = lambda value, axis, d: lax.ppermute(value, "col", shift[axis](d))
    got, own = [None, None], [None, None]
    far_in, near_in, stash = [None, None], [None, None], [None, None]
    for axis in (0, 1):
        up, down = far(axis, meta, a, ap, integrals, v1)
        far_in[axis] = send(up, axis, 1), send(down, axis, -1)
    for axis in (0, 1):
        up, down, up_st, down_st = near(axis, meta, a, ap, integrals, v1, v2)
        near_in[axis] = send(down, axis, -1), send(up, axis, 1)
        stash[axis] = up_st, down_st
    homes = [home(axis, meta, a, ap, integrals, v1, v2) for axis in (0, 1)]
    last = [None, None]
    for axis in (0, 1):
        up, down = relay("relay_y" if axis else "relay_x", *far_in[axis], *stash[axis])
        last[axis] = send(up, axis, 1), send(down, axis, -1)
    for axis in (0, 1):
        own[axis], m1, m2, m3 = turn(
            "turn_y" if axis else "turn_x", homes[axis], near_in[axis][0], last[axis][0], near_in[axis][1], last[axis][1]
        )
        got[axis] = send(m2, 1 - axis, 2), send(m1, 1 - axis, 1), send(m3, 1 - axis, -1)
    holes = jnp.dot(hole_integrals, gathered, preferred_element_type=F32)
    return finish(own[0], own[1], got[0], got[1], holes, occupied_energy, virtual_energy)


def solution(mesh):
    return jax.shard_map(
        shards,
        mesh=mesh,
        in_specs=(
            P("row", ("col", "layer")),
            P(("col", "layer"), None),
            P("row", None),
            P(),
            P("row"),
            P(("col", "layer")),
        ),
        out_specs=P("row", ("col", "layer")),
        check_vma=False,
    )
```

```python
import jax
import jax.numpy as jnp
from jax import lax
from jax.experimental import pallas as pl
from jax.experimental.pallas import tpu as pltpu
from jax.sharding import PartitionSpec as P

TB = 128
X = 4
Y = 4
F32 = jnp.float32
I16 = jnp.int16
I32 = jnp.int32
BF16 = jnp.bfloat16
TOP = 32700.0
STEPS = 64.0
SCALE = 1000
VMEM = 10 * 1024 * 1024
SM = pl.BlockSpec(memory_space=pltpu.SMEM)
VM = pl.BlockSpec(memory_space=pltpu.VMEM)
ANY = pl.BlockSpec(memory_space=pl.ANY)

FAR, NEAR, HOME, ALL = (0, 4), (4, 8), (12, 4), (0, 16)


def hop(first, d):
    pairs = []
    for y in range(Y):
        for x in range(X):
            for layer in range(2):
                along_x = (layer == 0) == first
                to = (y * X + (x + d) % X) if along_x else ((y + d) % Y * X + x)
                pairs.append(((y * X + x) * 2 + layer, to * 2 + layer))
    return pairs


def send(value, first, d):
    return lax.ppermute(value, ("col", "layer"), hop(first, d))


def inside(value):
    return pltpu.with_memory_space_constraint(value, pltpu.VMEM)


def params():
    return pltpu.CompilerParams(vmem_limit_bytes=VMEM)


def cost(flops, moved):
    return pl.CostEstimate(flops=int(flops) // SCALE, bytes_accessed=int(moved) // SCALE, transcendentals=0)


def loop(n, unroll=1):
    def run(step):
        lax.fori_loop(0, n, lambda i, c: (step(i), c)[1], 0, unroll=unroll)
    return run


def rows_at(i, n):
    return pl.ds(pl.multiple_of(i * n, n), n)


def encode(block):
    peak = jnp.maximum(jnp.max(jnp.abs(block), axis=0, keepdims=True), 1e-30)
    code = jnp.floor(jnp.log2(TOP / peak) * STEPS)
    scale = jnp.exp2(code * (1.0 / STEPS))
    return jnp.round(block * scale).astype(I32).astype(I16), code


def put(ref, k, block):
    coded, code = encode(block)
    ref[rows_at(k, TB), :] = coded
    last = slice(ref.shape[0] - 16, ref.shape[0])
    rows = ref[last, :].astype(I32)
    at = lax.broadcasted_iota(I32, rows.shape, 0) == k
    ref[last, :] = jnp.where(at, code.astype(I32), rows).astype(I16)


def get(ref, k):
    rows = ref[ref.shape[0] - 16:, :].astype(I32)
    at = lax.broadcasted_iota(I32, rows.shape, 0) == k
    code = jnp.sum(jnp.where(at, rows, 0).astype(F32), axis=0, keepdims=True)
    scale = jnp.exp2(code * (1.0 / STEPS))
    return ref[rows_at(k, TB), :].astype(I32).astype(F32) * (1.0 / scale)


def pack(name, mask, integrals, parts, after=()):
    width = integrals.shape[0]
    tiles = width // TB
    total = sum(n for _, n, _ in parts)

    def body(mask_ref, v_ref, *refs):
        outs, (mask_s, sem, mask_sem) = refs[len(after):-3], refs[-3:]
        mask_copy = pltpu.make_async_copy(mask_ref, mask_s, mask_sem)
        mask_copy.start()
        col, layer = lax.axis_index("col"), lax.axis_index("layer")
        x, y = lax.rem(col, X), lax.div(col, X)
        row = (col * 2 + layer) * tiles

        def source(place, mine):
            who = layer if mine else 1 - layer
            d, o = jnp.right_shift(place, 2), jnp.bitwise_and(place, 3)
            d = jnp.where(d == 0, 2, jnp.where(d == 1, 1, jnp.where(d == 2, 3, 0)))
            dx, dy = jnp.where(who == 0, d, o), jnp.where(who == 0, o, d)
            return (lax.rem(y + dy, Y) * X + lax.rem(x + dx, X)) * 2 + who

        def copy(out, k, at, slot):
            return pltpu.make_async_copy(
                v_ref.at[:, pl.ds(pl.multiple_of(at * width, width), width)], out.at[k], sem.at[slot]
            )

        slots = [sum(n for _, n, _ in parts[:p]) for p in range(len(parts))]
        for (start, n, mine), out, slot in zip(parts, outs, slots):
            @loop(n)
            def _(k):
                copy(out, k, source(start + k, mine), slot + k).start()
        mask_copy.wait()
        for (start, n, mine), out, slot in zip(parts, outs, slots):
            @loop(n)
            def _(k):
                at = source(start + k, mine)
                copy(out, k, at, slot + k).wait()
                for kt in range(tiles):
                    for qt in range(tiles):
                        here = (k, slice(kt * TB, (kt + 1) * TB), slice(qt * TB, (qt + 1) * TB))

                        @pl.when(mask_s[row + kt, at * tiles + qt] == 0)
                        def _():
                            out[here] = jnp.zeros((TB, TB), BF16)

    return pl.pallas_call(
        body,
        out_shape=[pltpu.VMEM((n, width, width), BF16) for _, n, _ in parts],
        in_specs=[ANY, ANY] + [ANY] * len(after),
        out_specs=[VM] * len(parts),
        scratch_shapes=[pltpu.SMEM(mask.shape, I32), pltpu.SemaphoreType.DMA((total,)), pltpu.SemaphoreType.DMA(())],
        compiler_params=params(),
        cost_estimate=cost(0, 4 * total * width * width),
        name=name,
    )(*(pltpu.with_memory_space_constraint(v, pltpu.HBM) for v in (mask, integrals)), *after)


def product(lhs, own_ref, k, their_ref, their_k):
    return jnp.dot(lhs, jnp.concatenate([own_ref[k], their_ref[their_k]], axis=0), preferred_element_type=F32)


def left(a_ref, ap_ref):
    return jnp.concatenate([a_ref[...], ap_ref[...]], axis=1)


def far(a, ap, own_v, v1):
    rows, width = a.shape
    half = rows // 2
    n = half // TB
    msg = 4 * half + 16

    def body(a_ref, ap_ref, own_ref, v1_ref, up_ref, down_ref):
        lhs = left(a_ref, ap_ref)

        @loop(4)
        def _(o):
            part = product(lhs, own_ref, o, v1_ref, o)
            for b in range(n):
                put(up_ref, o * n + b, part[b * TB:(b + 1) * TB])
                put(down_ref, o * n + b, part[half + b * TB:half + (b + 1) * TB])

    return pl.pallas_call(
        body,
        out_shape=[pltpu.VMEM((msg, width), I16)] * 2,
        in_specs=[VM] * 4,
        out_specs=[VM] * 2,
        compiler_params=params(),
        cost_estimate=cost(2 * 4 * rows * 2 * width * width, 4 * 4 * width * width),
        name="far",
    )(*map(inside, (a, ap, own_v, v1)))


def near(a, ap, own_v, v2):
    rows, width = a.shape
    half = rows // 2
    n = half // TB
    msg = 4 * half + 16

    def body(a_ref, ap_ref, own_ref, v2_ref, up_ref, down_ref, up_st, down_st):
        lhs = left(a_ref, ap_ref)

        @loop(4)
        def _(o):
            part = product(lhs, own_ref, 4 + o, v2_ref, o)
            up_st[rows_at(o, half), :] = part[:half]
            for b in range(n):
                put(up_ref, o * n + b, part[half + b * TB:half + (b + 1) * TB])
            part = product(lhs, own_ref, 8 + o, v2_ref, 4 + o)
            down_st[rows_at(o, half), :] = part[half:]
            for b in range(n):
                put(down_ref, o * n + b, part[b * TB:(b + 1) * TB])

    return pl.pallas_call(
        body,
        out_shape=[pltpu.VMEM((msg, width), I16)] * 2 + [pltpu.VMEM((4 * half, width), F32)] * 2,
        in_specs=[VM] * 4,
        out_specs=[VM] * 4,
        compiler_params=params(),
        cost_estimate=cost(2 * 8 * rows * 2 * width * width, 8 * 4 * width * width),
        name="near",
    )(*map(inside, (a, ap, own_v, v2)))


def home(a, ap, own_v, v2, near_up, near_down):
    rows, width = a.shape
    n = rows // TB
    h = n // 2

    def body(a_ref, ap_ref, own_ref, v2_ref, up_ref, down_ref, out_ref):
        lhs = left(a_ref, ap_ref)

        @loop(4)
        def _(o):
            part = product(lhs, own_ref, 12 + o, v2_ref, o)
            for b in range(n):
                here = slice(b * TB, (b + 1) * TB)
                out_ref[o, here, :] = part[here] + get(up_ref if b < h else down_ref, o * h + b % h)

    return pl.pallas_call(
        body,
        out_shape=pltpu.VMEM((4, rows, width), F32),
        in_specs=[VM] * 6,
        out_specs=VM,
        compiler_params=params(),
        cost_estimate=cost(2 * 4 * rows * 2 * width * width, 4 * 4 * width * width),
        name="home",
    )(*map(inside, (a, ap, own_v, v2, near_up, near_down)))


def relay(got, own):
    rows, width = own.shape

    def body(got_ref, own_ref, out_ref):
        @loop(rows // TB)
        def _(k):
            put(out_ref, k, own_ref[rows_at(k, TB), :] + get(got_ref, k))

    return pl.pallas_call(
        body,
        out_shape=pltpu.VMEM(got.shape, I16),
        in_specs=[VM] * 2,
        out_specs=VM,
        compiler_params=params(),
        cost_estimate=cost(0, 8 * rows * width),
        name="relay",
    )(*map(inside, (got, own)))


def turn(st, far_up, far_down):
    _, rows, width = st.shape
    n = rows // TB
    h = n // 2

    def body(st_ref, up_ref, down_ref, own_ref, m1_ref, m2_ref, m3_ref):
        for o, ref in ((2, m2_ref), (1, m1_ref), (3, m3_ref), (0, own_ref)):
            for b in range(n):
                part = st_ref[o, b * TB:(b + 1) * TB, :] + get(up_ref if b < h else down_ref, o * h + b % h)
                if o == 0:
                    ref[b * TB:(b + 1) * TB, :] = part
                else:
                    put(ref, b, part)

    return pl.pallas_call(
        body,
        out_shape=[pltpu.VMEM((rows, width), F32)] + [pltpu.VMEM((rows + 16, width), I16)] * 3,
        in_specs=[VM] * 3,
        out_specs=[VM] * 4,
        compiler_params=params(),
        cost_estimate=cost(0, 4 * rows * width * 10),
        name="turn",
    )(*map(inside, (st, far_up, far_down)))


def hole_sum(hole_integrals, gathered):
    rows, depth = hole_integrals.shape
    width = gathered.shape[1]
    parts = 8
    step = depth // parts

    def body(h_hbm, a_hbm, out_ref, h_ref, a_ref, sem):
        copies = []
        for i in range(parts):
            here = slice(i * step, (i + 1) * step)
            pair = (
                pltpu.make_async_copy(h_hbm.at[:, here], h_ref.at[i], sem.at[0, i]),
                pltpu.make_async_copy(a_hbm.at[here, :], a_ref.at[i], sem.at[1, i]),
            )
            for copy in pair:
                copy.start()
            copies.append(pair)
        for i in range(parts):
            for copy in copies[i]:
                copy.wait()
            part = jnp.dot(h_ref[i], a_ref[i], preferred_element_type=F32)
            out_ref[...] = part if i == 0 else out_ref[...] + part

    return pl.pallas_call(
        body,
        out_shape=pltpu.VMEM((rows, width), F32),
        in_specs=[ANY] * 2,
        out_specs=VM,
        scratch_shapes=[
            pltpu.VMEM((parts, rows, step), BF16),
            pltpu.VMEM((parts, step, width), BF16),
            pltpu.SemaphoreType.DMA((2, parts)),
        ],
        compiler_params=params(),
        cost_estimate=cost(2 * rows * depth * width, 2 * depth * (rows + width)),
        name="holes",
    )(*(pltpu.with_memory_space_constraint(v, pltpu.HBM) for v in (hole_integrals, gathered)))


def finish(own, got, holes, occupied, virtual):
    rows, width = own.shape

    def body(own_ref, m1, m2, m3, holes_ref, occ_ref, virt_ref, out_ref):
        virt = virt_ref[...]
        for b in range(rows // TB):
            here = slice(b * TB, (b + 1) * TB)
            total = own_ref[here, :] + get(m1, b) + get(m2, b) + get(m3, b)
            occ = jnp.broadcast_to(occ_ref[:, here], (TB, TB)).T
            occ = jnp.concatenate([occ] * (width // TB), axis=1)
            out_ref[here, :] = (total + holes_ref[here, :]) / (virt - occ)

    return pl.pallas_call(
        body,
        out_shape=jax.ShapeDtypeStruct((rows, width), F32),
        in_specs=[VM] * 7,
        out_specs=VM,
        compiler_params=params(),
        cost_estimate=cost(0, 4 * rows * width * 6),
        name="finish",
    )(own, *got, holes, occupied[None, :], virtual[None, :])


def shards(amplitudes, integrals, hole_integrals, tile_mask, occupied_energy, virtual_energy):
    swap = [(0, 1), (1, 0)]
    gathered = lax.all_gather(amplitudes, "row", axis=0, tiled=True)
    a, ap = amplitudes, lax.ppermute(amplitudes, "layer", swap)
    first, second = pack("pack_far_near", tile_mask, integrals, [(*FAR, False), (*NEAR, False)])
    v1 = lax.ppermute(first, "layer", swap)
    v2 = lax.ppermute(second, "layer", swap)
    own_v, third = pack("pack_own_home", tile_mask, integrals, [(*ALL, True), (*HOME, False)], [first])
    v3 = lax.ppermute(third, "layer", swap)

    up, down = far(a, ap, own_v, v1)
    far_up, far_down = send(up, True, 1), send(down, True, -1)
    up, down, up_st, down_st = near(a, ap, own_v, v2)
    near_down, near_up = send(up, True, 1), send(down, True, -1)
    up = relay(far_up, up_st)
    far_up = send(up, True, 1)
    down = relay(far_down, down_st)
    far_down = send(down, True, -1)
    st = home(a, ap, own_v, v3, near_up, near_down)
    own, m1, m2, m3 = turn(st, far_up, far_down)
    got = send(m2, False, 2), send(m1, False, 1), send(m3, False, -1)
    holes = hole_sum(hole_integrals, gathered)
    return finish(own, got, holes, occupied_energy, virtual_energy)


def solution(mesh):
    return jax.shard_map(
        shards,
        mesh=mesh,
        in_specs=(
            P("row", ("col", "layer")),
            P(("col", "layer"), None),
            P("row", None),
            P(),
            P("row"),
            P(("col", "layer")),
        ),
        out_specs=P("row", ("col", "layer")),
        check_vma=False,
    )
```

```python
import jax
import jax.numpy as jnp
from jax import lax
from jax.experimental import pallas as pl
from jax.experimental.pallas import tpu as pltpu
from jax.sharding import PartitionSpec as P

TB = 128
X = 4
Y = 4
F32 = jnp.float32
I16 = jnp.int16
I32 = jnp.int32
BF16 = jnp.bfloat16
TOP = 32700.0
STEPS = 64.0
SCALE = 1000
VMEM = 10 * 1024 * 1024
SM = pl.BlockSpec(memory_space=pltpu.SMEM)
VM = pl.BlockSpec(memory_space=pltpu.VMEM)
ANY = pl.BlockSpec(memory_space=pl.ANY)

FAR, REST, ALL = (0, 4), (4, 12), (0, 16)


def hop(first, d):
    pairs = []
    for y in range(Y):
        for x in range(X):
            for layer in range(2):
                along_x = (layer == 0) == first
                to = (y * X + (x + d) % X) if along_x else ((y + d) % Y * X + x)
                pairs.append(((y * X + x) * 2 + layer, to * 2 + layer))
    return pairs


def send(value, first, d):
    return lax.ppermute(value, ("col", "layer"), hop(first, d))


def run(body, after, operands, in_specs, out_shape, out_specs, carry=(), **kw):
    n, m, c = len(operands), len(after), len(carry)
    single = not isinstance(out_shape, list)
    shapes, specs = ([out_shape], [out_specs]) if single else (out_shape, out_specs)
    k = len(shapes)

    def whole(*refs):
        ins, outs = refs[:n + c + m], refs[n + c + m:]
        for i in range(c):
            outs[k + i][...] = ins[n + i][...]
        body(*ins[:n], *outs[:k], *outs[k + c:])

    out = pl.pallas_call(
        whole,
        in_specs=list(in_specs) + [VM] * c + [ANY] * m,
        out_shape=list(shapes) + [pltpu.VMEM(v.shape, v.dtype) for v in carry],
        out_specs=list(specs) + [VM] * c,
        compiler_params=params(),
        **kw,
    )(*operands, *map(inside, carry), *after)
    return out[0] if single and not c else out


def inside(value):
    return pltpu.with_memory_space_constraint(value, pltpu.VMEM)


def params():
    return pltpu.CompilerParams(vmem_limit_bytes=VMEM)


def cost(flops, moved):
    return pl.CostEstimate(flops=int(flops) // SCALE, bytes_accessed=int(moved) // SCALE, transcendentals=0)


LONG = cost(10 ** 14, 0)


def loop(n, unroll=1):
    def run(step):
        lax.fori_loop(0, n, lambda i, c: (step(i), c)[1], 0, unroll=unroll)
    return run


def rows_at(i, n):
    return pl.ds(pl.multiple_of(i * n, n), n)


def encode(block):
    peak = jnp.maximum(jnp.max(jnp.abs(block), axis=0, keepdims=True), 1e-30)
    code = jnp.floor(jnp.log2(TOP / peak) * STEPS)
    scale = jnp.exp2(code * (1.0 / STEPS))
    return jnp.round(block * scale).astype(I32).astype(I16), code


def put(ref, k, block):
    coded, code = encode(block)
    ref[rows_at(k, TB), :] = coded
    last = slice(ref.shape[0] - 16, ref.shape[0])
    rows = ref[last, :].astype(I32)
    at = lax.broadcasted_iota(I32, rows.shape, 0) == k
    ref[last, :] = jnp.where(at, code.astype(I32), rows).astype(I16)


def get(ref, k):
    rows = ref[ref.shape[0] - 16:, :].astype(I32)
    at = lax.broadcasted_iota(I32, rows.shape, 0) == k
    code = jnp.sum(jnp.where(at, rows, 0).astype(F32), axis=0, keepdims=True)
    scale = jnp.exp2(code * (1.0 / STEPS))
    return ref[rows_at(k, TB), :].astype(I32).astype(F32) * (1.0 / scale)


def pack(name, mask, integrals, parts, after=()):
    width = integrals.shape[0]
    tiles = width // TB
    total = sum(n for _, n, _ in parts)

    def body(mask_ref, v_ref, *refs):
        outs, (mask_s, sem, mask_sem) = refs[len(after):-3], refs[-3:]
        mask_copy = pltpu.make_async_copy(mask_ref, mask_s, mask_sem)
        mask_copy.start()
        col, layer = lax.axis_index("col"), lax.axis_index("layer")
        x, y = lax.rem(col, X), lax.div(col, X)
        row = (col * 2 + layer) * tiles

        def source(place, mine):
            who = layer if mine else 1 - layer
            d, o = jnp.right_shift(place, 2), jnp.bitwise_and(place, 3)
            d = jnp.where(d == 0, 2, jnp.where(d == 1, 1, jnp.where(d == 2, 3, 0)))
            dx, dy = jnp.where(who == 0, d, o), jnp.where(who == 0, o, d)
            return (lax.rem(y + dy, Y) * X + lax.rem(x + dx, X)) * 2 + who

        def copy(out, k, at, slot):
            return pltpu.make_async_copy(
                v_ref.at[:, pl.ds(pl.multiple_of(at * width, width), width)], out.at[k], sem.at[slot]
            )

        slots = [sum(n for _, n, _ in parts[:p]) for p in range(len(parts))]
        for (start, n, mine), out, slot in zip(parts, outs, slots):
            @loop(n)
            def _(k):
                copy(out, k, source(start + k, mine), slot + k).start()
        mask_copy.wait()
        for (start, n, mine), out, slot in zip(parts, outs, slots):
            @loop(n)
            def _(k):
                at = source(start + k, mine)
                copy(out, k, at, slot + k).wait()
                for kt in range(tiles):
                    for qt in range(tiles):
                        here = (k, slice(kt * TB, (kt + 1) * TB), slice(qt * TB, (qt + 1) * TB))

                        @pl.when(mask_s[row + kt, at * tiles + qt] == 0)
                        def _():
                            out[here] = jnp.zeros((TB, TB), BF16)

    return pl.pallas_call(
        body,
        out_shape=[pltpu.VMEM((n, width, width), BF16) for _, n, _ in parts],
        in_specs=[ANY, ANY] + [ANY] * len(after),
        out_specs=[VM] * len(parts),
        scratch_shapes=[pltpu.SMEM(mask.shape, I32), pltpu.SemaphoreType.DMA((total,)), pltpu.SemaphoreType.DMA(())],
        compiler_params=params(),
        cost_estimate=cost(0, 4 * total * width * width),
        name=name,
    )(*(pltpu.with_memory_space_constraint(v, pltpu.HBM) for v in (mask, integrals)), *after)


def product(lhs, own_ref, k, their_ref, their_k):
    return jnp.dot(lhs, jnp.concatenate([own_ref[k], their_ref[their_k]], axis=0), preferred_element_type=F32)


def left(a_ref, ap_ref):
    return jnp.concatenate([a_ref[...], ap_ref[...]], axis=1)


def hand_on(blocks, after, estimate=cost(0, 0)):
    return run(lambda: None, after, [], [], [], [], blocks, cost_estimate=estimate, name="hand_on")


def far(a, ap, own_v, v1, after=(), carry=()):
    rows, width = a.shape
    half = rows // 2
    n = half // TB
    msg = 4 * half + 16

    def body(a_ref, ap_ref, own_ref, v1_ref, up_ref, down_ref):
        lhs = left(a_ref, ap_ref)

        @loop(4)
        def _(o):
            part = product(lhs, own_ref, o, v1_ref, o)
            for b in range(n):
                put(up_ref, o * n + b, part[b * TB:(b + 1) * TB])
                put(down_ref, o * n + b, part[half + b * TB:half + (b + 1) * TB])

    return run(
        body,
        after,
        [*map(inside, (a, ap, own_v, v1))],
        [VM] * 4,
        out_shape=[pltpu.VMEM((msg, width), I16)] * 2,
        out_specs=[VM] * 2,
        cost_estimate=cost(2 * 4 * rows * 2 * width * width, 4 * 4 * width * width),
        carry=carry,
        name="far",
    )


def near(a, ap, own_v, v2, after=(), carry=()):
    rows, width = a.shape
    half = rows // 2
    n = half // TB
    msg = 4 * half + 16

    def body(a_ref, ap_ref, own_ref, v2_ref, up_ref, down_ref, up_st, down_st):
        lhs = left(a_ref, ap_ref)

        @loop(4)
        def _(o):
            part = product(lhs, own_ref, 4 + o, v2_ref, o)
            up_st[rows_at(o, half), :] = part[:half]
            for b in range(n):
                put(up_ref, o * n + b, part[half + b * TB:half + (b + 1) * TB])
            part = product(lhs, own_ref, 8 + o, v2_ref, 4 + o)
            down_st[rows_at(o, half), :] = part[half:]
            for b in range(n):
                put(down_ref, o * n + b, part[b * TB:(b + 1) * TB])

    return run(
        body,
        after,
        [*map(inside, (a, ap, own_v, v2))],
        [VM] * 4,
        out_shape=[pltpu.VMEM((msg, width), I16)] * 2 + [pltpu.VMEM((4 * half, width), F32)] * 2,
        out_specs=[VM] * 4,
        cost_estimate=LONG,
        carry=carry,
        name="near",
    )


def home(a, ap, own_v, v2, near_up, near_down, after=(), carry=()):
    rows, width = a.shape
    n = rows // TB
    h = n // 2

    def body(a_ref, ap_ref, own_ref, v2_ref, up_ref, down_ref, out_ref):
        lhs = left(a_ref, ap_ref)

        @loop(4)
        def _(o):
            part = product(lhs, own_ref, 12 + o, v2_ref, 8 + o)
            for b in range(n):
                here = slice(b * TB, (b + 1) * TB)
                out_ref[o, here, :] = part[here] + get(up_ref if b < h else down_ref, o * h + b % h)

    return run(
        body,
        after,
        [*map(inside, (a, ap, own_v, v2, near_up, near_down))],
        [VM] * 6,
        out_shape=pltpu.VMEM((4, rows, width), F32),
        out_specs=VM,
        cost_estimate=LONG,
        carry=carry,
        name="home",
    )


def relay(got, own, after=(), carry=()):
    rows, width = own.shape

    def body(got_ref, own_ref, out_ref):
        @loop(rows // TB)
        def _(k):
            put(out_ref, k, own_ref[rows_at(k, TB), :] + get(got_ref, k))

    return run(
        body,
        after,
        [*map(inside, (got, own))],
        [VM] * 2,
        out_shape=pltpu.VMEM(got.shape, I16),
        out_specs=VM,
        cost_estimate=cost(0, 8 * rows * width),
        carry=carry,
        name="relay",
    )


def turn(st, far_up, far_down, after=(), carry=()):
    _, rows, width = st.shape
    n = rows // TB
    h = n // 2

    def body(st_ref, up_ref, down_ref, own_ref, m1_ref, m2_ref, m3_ref):
        for o, ref in ((2, m2_ref), (1, m1_ref), (3, m3_ref), (0, own_ref)):
            for b in range(n):
                part = st_ref[o, b * TB:(b + 1) * TB, :] + get(up_ref if b < h else down_ref, o * h + b % h)
                if o == 0:
                    ref[b * TB:(b + 1) * TB, :] = part
                else:
                    put(ref, b, part)

    return run(
        body,
        after,
        [*map(inside, (st, far_up, far_down))],
        [VM] * 3,
        out_shape=[pltpu.VMEM((rows, width), F32)] + [pltpu.VMEM((rows + 16, width), I16)] * 3,
        out_specs=[VM] * 4,
        cost_estimate=cost(0, 4 * rows * width * 10),
        carry=carry,
        name="turn",
    )


def hole_part(name, hole_integrals, blocks, away, before=None, after=()):
    rows = hole_integrals.shape[0]
    depth, width = blocks[0].shape
    count = hole_integrals.shape[1] // depth
    more = [] if before is None else [before]

    def body(h_ref, *refs):
        out_ref = refs[-1]
        here = lax.axis_index("row")
        total = refs[len(blocks)][...] if more else None
        for ref, k in zip(refs, away):
            at = lax.rem(here + (k + count), count)
            part = jnp.dot(h_ref[:, rows_at(at, depth)], ref[...], preferred_element_type=F32)
            total = part if total is None else total + part
        out_ref[...] = total

    return run(
        body,
        after,
        [*map(inside, (hole_integrals, *blocks, *more))],
        [VM] * (1 + len(blocks) + len(more)),
        out_shape=pltpu.VMEM((rows, width), F32),
        out_specs=VM,
        cost_estimate=LONG,
        name=name,
    )


def finish(own, got, holes, occupied, virtual):
    rows, width = own.shape

    def body(own_ref, m1, m2, m3, holes_ref, occ_ref, virt_ref, out_ref):
        virt = virt_ref[...]
        for b in range(rows // TB):
            here = slice(b * TB, (b + 1) * TB)
            total = own_ref[here, :] + get(m1, b) + get(m2, b) + get(m3, b)
            occ = jnp.broadcast_to(occ_ref[:, here], (TB, TB)).T
            occ = jnp.concatenate([occ] * (width // TB), axis=1)
            out_ref[here, :] = (total + holes_ref[here, :]) / (virt - occ)

    return pl.pallas_call(
        body,
        out_shape=jax.ShapeDtypeStruct((rows, width), F32),
        in_specs=[VM] * 7,
        out_specs=VM,
        compiler_params=params(),
        cost_estimate=cost(0, 4 * rows * width * 6),
        name="finish",
    )(own, *got, holes, occupied[None, :], virtual[None, :])


def shards(amplitudes, integrals, hole_integrals, tile_mask, occupied_energy, virtual_energy):
    swap = [(0, 1), (1, 0)]
    z = lax.axis_size("row")
    a = amplitudes

    def ring(value, d):
        return lax.ppermute(value, "row", [(i, (i + d) % z) for i in range(z)])

    first, second = pack("pack_theirs", tile_mask, integrals, [(*FAR, False), (*REST, False)])
    v1 = lax.ppermute(first, "layer", swap)
    ap = lax.ppermute(a, "layer", swap)
    high, low = [ring(a, 1)], [ring(a, -1)]
    v2 = lax.ppermute(second, "layer", swap)
    [own_v] = pack("pack_own", tile_mask, integrals, [(*ALL, True)], [first])

    up, down = far(a, ap, own_v, v1)
    far_up, far_down = send(up, True, 1), send(down, True, -1)
    here = hand_on([high[0], low[0]], [up])
    high.append(ring(here[0], 1))
    low.append(ring(here[1], -1))
    up, down, up_st, down_st = near(a, ap, own_v, v2, here)
    near_down, near_up = send(up, True, 1), send(down, True, -1)
    up = relay(far_up, up_st)
    far_up = send(up, True, 1)
    down = relay(far_down, down_st, [up])
    far_down = send(down, True, -1)
    here = hand_on([high[1], low[1]], [down], LONG)
    high.append(ring(here[0], 1))
    low.append(ring(here[1], -1))
    st = home(a, ap, own_v, v2, near_up, near_down, here)
    here = hand_on([high[2]], [st])
    high.append(ring(here[0], 1))
    own, m1, m2, m3 = turn(st, far_up, far_down, here)
    got = send(m2, False, 2), send(m1, False, 1), send(m3, False, -1)
    low[2:] = hand_on(low[2:], [m1, m2, m3])
    holes = hole_part("holes", hole_integrals, [a, *high, *low], [0, -1, -2, -3, -4, 1, 2, 3], None, [m1, m2, m3])
    return finish(own, got, holes, occupied_energy, virtual_energy)


def solution(mesh):
    return jax.shard_map(
        shards,
        mesh=mesh,
        in_specs=(
            P("row", ("col", "layer")),
            P(("col", "layer"), None),
            P("row", None),
            P(),
            P("row"),
            P(("col", "layer")),
        ),
        out_specs=P("row", ("col", "layer")),
        check_vma=False,
    )
```

```python
import jax
import jax.numpy as jnp
from jax import lax
from jax.experimental import pallas as pl
from jax.experimental.pallas import tpu as pltpu
from jax.sharding import PartitionSpec as P

TB = 128
X = 4
Y = 4
F32 = jnp.float32
I16 = jnp.int16
I32 = jnp.int32
BF16 = jnp.bfloat16
TOP = 32700.0
STEPS = 64.0
SCALE = 1000
VMEM = 10 * 1024 * 1024
SM = pl.BlockSpec(memory_space=pltpu.SMEM)
VM = pl.BlockSpec(memory_space=pltpu.VMEM)
ANY = pl.BlockSpec(memory_space=pl.ANY)

FAR, REST = (0, 4), (4, 12)


def hop(first, d):
    pairs = []
    for y in range(Y):
        for x in range(X):
            for layer in range(2):
                along_x = (layer == 0) == first
                to = (y * X + (x + d) % X) if along_x else ((y + d) % Y * X + x)
                pairs.append(((y * X + x) * 2 + layer, to * 2 + layer))
    return pairs


def send(value, first, d):
    return lax.ppermute(value, ("col", "layer"), hop(first, d))


def run(body, after, operands, in_specs, out_shape, out_specs, carry=(), **kw):
    n, m, c = len(operands), len(after), len(carry)
    single = not isinstance(out_shape, list)
    shapes, specs = ([out_shape], [out_specs]) if single else (out_shape, out_specs)
    k = len(shapes)

    def whole(*refs):
        ins, outs = refs[:n + c + m], refs[n + c + m:]
        for i in range(c):
            outs[k + i][...] = ins[n + i][...]
        body(*ins[:n], *outs[:k], *outs[k + c:])

    out = pl.pallas_call(
        whole,
        in_specs=list(in_specs) + [VM] * c + [ANY] * m,
        out_shape=list(shapes) + [pltpu.VMEM(v.shape, v.dtype) for v in carry],
        out_specs=list(specs) + [VM] * c,
        compiler_params=params(),
        **kw,
    )(*operands, *map(inside, carry), *after)
    return out[0] if single and not c else out


def inside(value):
    return pltpu.with_memory_space_constraint(value, pltpu.VMEM)


def params():
    return pltpu.CompilerParams(vmem_limit_bytes=VMEM)


def cost(flops, moved):
    return pl.CostEstimate(flops=int(flops) // SCALE, bytes_accessed=int(moved) // SCALE, transcendentals=0)


LONG = cost(2 * 10 ** 13, 0)


def loop(n, unroll=1):
    def run(step):
        lax.fori_loop(0, n, lambda i, c: (step(i), c)[1], 0, unroll=unroll)
    return run


def rows_at(i, n):
    return pl.ds(pl.multiple_of(i * n, n), n)


def encode(block):
    peak = jnp.maximum(jnp.max(jnp.abs(block), axis=0, keepdims=True), 1e-30)
    code = jnp.floor(jnp.log2(TOP / peak) * STEPS)
    scale = jnp.exp2(code * (1.0 / STEPS))
    return jnp.round(block * scale).astype(I32).astype(I16), code


def put(ref, k, block):
    coded, code = encode(block)
    ref[rows_at(k, TB), :] = coded
    last = slice(ref.shape[0] - 16, ref.shape[0])
    rows = ref[last, :].astype(I32)
    at = lax.broadcasted_iota(I32, rows.shape, 0) == k
    ref[last, :] = jnp.where(at, code.astype(I32), rows).astype(I16)


def get(ref, k):
    rows = ref[ref.shape[0] - 16:, :].astype(I32)
    at = lax.broadcasted_iota(I32, rows.shape, 0) == k
    code = jnp.sum(jnp.where(at, rows, 0).astype(F32), axis=0, keepdims=True)
    scale = jnp.exp2(code * (1.0 / STEPS))
    return ref[rows_at(k, TB), :].astype(I32).astype(F32) * (1.0 / scale)


def pack(name, mask, integrals, parts, after=()):
    width = integrals.shape[0]
    tiles = width // TB
    total = sum(n for _, n, _ in parts)

    def body(mask_ref, v_ref, *refs):
        outs, (mask_s, sem, mask_sem) = refs[len(after):-3], refs[-3:]
        mask_copy = pltpu.make_async_copy(mask_ref, mask_s, mask_sem)
        mask_copy.start()
        col, layer = lax.axis_index("col"), lax.axis_index("layer")
        x, y = lax.rem(col, X), lax.div(col, X)
        row = (col * 2 + layer) * tiles

        def source(place, mine):
            who = layer if mine else 1 - layer
            d, o = jnp.right_shift(place, 2), jnp.bitwise_and(place, 3)
            d = jnp.where(d == 0, 2, jnp.where(d == 1, 1, jnp.where(d == 2, 3, 0)))
            dx, dy = jnp.where(who == 0, d, o), jnp.where(who == 0, o, d)
            return (lax.rem(y + dy, Y) * X + lax.rem(x + dx, X)) * 2 + who

        def copy(out, k, at, slot):
            return pltpu.make_async_copy(
                v_ref.at[:, pl.ds(pl.multiple_of(at * width, width), width)], out.at[k], sem.at[slot]
            )

        slots = [sum(n for _, n, _ in parts[:p]) for p in range(len(parts))]
        for (start, n, mine), out, slot in zip(parts, outs, slots):
            @loop(n)
            def _(k):
                copy(out, k, source(start + k, mine), slot + k).start()
        mask_copy.wait()
        for (start, n, mine), out, slot in zip(parts, outs, slots):
            @loop(n)
            def _(k):
                at = source(start + k, mine)
                copy(out, k, at, slot + k).wait()
                for kt in range(tiles):
                    for qt in range(tiles):
                        here = (k, slice(kt * TB, (kt + 1) * TB), slice(qt * TB, (qt + 1) * TB))

                        @pl.when(mask_s[row + kt, at * tiles + qt] == 0)
                        def _():
                            out[here] = jnp.zeros((TB, TB), BF16)

    return pl.pallas_call(
        body,
        out_shape=[pltpu.VMEM((n, width, width), BF16) for _, n, _ in parts],
        in_specs=[ANY, ANY] + [ANY] * len(after),
        out_specs=[VM] * len(parts),
        scratch_shapes=[pltpu.SMEM(mask.shape, I32), pltpu.SemaphoreType.DMA((total,)), pltpu.SemaphoreType.DMA(())],
        compiler_params=params(),
        cost_estimate=cost(0, 4 * total * width * width),
        name=name,
    )(*(pltpu.with_memory_space_constraint(v, pltpu.HBM) for v in (mask, integrals)), *after)


def product(lhs, own_ref, k, their_ref, their_k):
    return jnp.dot(lhs, jnp.concatenate([own_ref[k], their_ref[their_k]], axis=0), preferred_element_type=F32)


def left(a_ref, ap_ref):
    return jnp.concatenate([a_ref[...], ap_ref[...]], axis=1)


def hand_on(blocks, after, estimate=cost(0, 0)):
    return run(lambda: None, after, [], [], [], [], blocks, cost_estimate=estimate, name="hand_on")


def far(a, ap, own_v, v1, after=(), carry=()):
    rows, width = a.shape
    half = rows // 2
    n = half // TB
    msg = 4 * half + 16

    def body(a_ref, ap_ref, own_ref, v1_ref, up_ref, down_ref):
        lhs = left(a_ref, ap_ref)

        @loop(4)
        def _(o):
            part = product(lhs, own_ref, o, v1_ref, o)
            for b in range(n):
                put(up_ref, o * n + b, part[b * TB:(b + 1) * TB])
                put(down_ref, o * n + b, part[half + b * TB:half + (b + 1) * TB])

    return run(
        body,
        after,
        [*map(inside, (a, ap, own_v, v1))],
        [VM] * 4,
        out_shape=[pltpu.VMEM((msg, width), I16)] * 2,
        out_specs=[VM] * 2,
        cost_estimate=cost(2 * 4 * rows * 2 * width * width, 4 * 4 * width * width),
        carry=carry,
        name="far",
    )


def near(a, ap, own_v, v2, after=(), carry=()):
    rows, width = a.shape
    half = rows // 2
    n = half // TB
    msg = 4 * half + 16

    def body(a_ref, ap_ref, own_ref, v2_ref, up_ref, down_ref, up_st, down_st):
        lhs = left(a_ref, ap_ref)

        @loop(4)
        def _(o):
            part = product(lhs, own_ref, o, v2_ref, o)
            up_st[rows_at(o, half), :] = part[:half]
            for b in range(n):
                put(up_ref, o * n + b, part[half + b * TB:half + (b + 1) * TB])
            part = product(lhs, own_ref, 4 + o, v2_ref, 4 + o)
            down_st[rows_at(o, half), :] = part[half:]
            for b in range(n):
                put(down_ref, o * n + b, part[b * TB:(b + 1) * TB])

    return run(
        body,
        after,
        [*map(inside, (a, ap, own_v, v2))],
        [VM] * 4,
        out_shape=[pltpu.VMEM((msg, width), I16)] * 2 + [pltpu.VMEM((4 * half, width), F32)] * 2,
        out_specs=[VM] * 4,
        cost_estimate=LONG,
        carry=carry,
        name="near",
    )


def home(a, ap, own_v, v2, near_up, near_down, after=(), carry=()):
    rows, width = a.shape
    n = rows // TB
    h = n // 2

    def body(a_ref, ap_ref, own_ref, v2_ref, up_ref, down_ref, out_ref):
        lhs = left(a_ref, ap_ref)

        @loop(4)
        def _(o):
            part = product(lhs, own_ref, 8 + o, v2_ref, 8 + o)
            for b in range(n):
                here = slice(b * TB, (b + 1) * TB)
                out_ref[o, here, :] = part[here] + get(up_ref if b < h else down_ref, o * h + b % h)

    return run(
        body,
        after,
        [*map(inside, (a, ap, own_v, v2, near_up, near_down))],
        [VM] * 6,
        out_shape=pltpu.VMEM((4, rows, width), F32),
        out_specs=VM,
        cost_estimate=LONG,
        carry=carry,
        name="home",
    )


def relay(got, own, after=(), carry=()):
    rows, width = own.shape

    def body(got_ref, own_ref, out_ref):
        @loop(rows // TB)
        def _(k):
            put(out_ref, k, own_ref[rows_at(k, TB), :] + get(got_ref, k))

    return run(
        body,
        after,
        [*map(inside, (got, own))],
        [VM] * 2,
        out_shape=pltpu.VMEM(got.shape, I16),
        out_specs=VM,
        cost_estimate=cost(0, 8 * rows * width),
        carry=carry,
        name="relay",
    )


def turn(st, far_up, far_down, after=(), carry=()):
    _, rows, width = st.shape
    n = rows // TB
    h = n // 2

    def body(st_ref, up_ref, down_ref, own_ref, m1_ref, m2_ref, m3_ref):
        for o, ref in ((2, m2_ref), (1, m1_ref), (3, m3_ref), (0, own_ref)):
            for b in range(n):
                part = st_ref[o, b * TB:(b + 1) * TB, :] + get(up_ref if b < h else down_ref, o * h + b % h)
                if o == 0:
                    ref[b * TB:(b + 1) * TB, :] = part
                else:
                    put(ref, b, part)

    return run(
        body,
        after,
        [*map(inside, (st, far_up, far_down))],
        [VM] * 3,
        out_shape=[pltpu.VMEM((rows, width), F32)] + [pltpu.VMEM((rows + 16, width), I16)] * 3,
        out_specs=[VM] * 4,
        cost_estimate=cost(0, 4 * rows * width * 10),
        carry=carry,
        name="turn",
    )


def hole_part(hole_integrals, blocks, away, own, occupied, virtual, after=()):
    rows = hole_integrals.shape[0]
    depth, width = blocks[0].shape
    count = hole_integrals.shape[1] // depth

    def body(h_ref, own_ref, occ_ref, virt_ref, *refs):
        sum_ref, inverse_ref = refs[-2:]
        here = lax.axis_index("row")
        virt = virt_ref[...]
        for b in range(rows // TB):
            at = slice(b * TB, (b + 1) * TB)
            occ = jnp.broadcast_to(occ_ref[:, at], (TB, TB)).T
            inverse_ref[at, :] = 1.0 / (virt - jnp.concatenate([occ] * (width // TB), axis=1))
        total = own_ref[...]
        for ref, k in zip(refs, away):
            at = lax.rem(here + (k + count), count)
            total = total + jnp.dot(h_ref[:, rows_at(at, depth)], ref[...], preferred_element_type=F32)
        sum_ref[...] = total

    return run(
        body,
        after,
        [*map(inside, (hole_integrals, own)), occupied[None, :], virtual[None, :], *map(inside, blocks)],
        [VM] * (4 + len(blocks)),
        out_shape=[pltpu.VMEM((rows, width), F32)] * 2,
        out_specs=[VM] * 2,
        cost_estimate=LONG,
        name="holes",
    )


def finish(total, inverse, got):
    rows, width = total.shape
    n = rows // TB

    def body(sum_ref, inverse_ref, m1, m2, m3, out_hbm, out_ref, sem):
        copies = []
        for b in range(n):
            here = slice(b * TB, (b + 1) * TB)
            part = sum_ref[here, :] + get(m1, b) + get(m2, b) + get(m3, b)
            out_ref[here, :] = part * inverse_ref[here, :]
            copies.append(pltpu.make_async_copy(out_ref.at[here, :], out_hbm.at[here, :], sem.at[b]))
            copies[-1].start()
        for copy in copies:
            copy.wait()

    return pl.pallas_call(
        body,
        out_shape=jax.ShapeDtypeStruct((rows, width), F32),
        in_specs=[VM] * 5,
        out_specs=ANY,
        scratch_shapes=[pltpu.VMEM((rows, width), F32), pltpu.SemaphoreType.DMA((n,))],
        compiler_params=params(),
        cost_estimate=cost(0, 4 * rows * width * 6),
        name="finish",
    )(*map(inside, (total, inverse, *got)))


def shards(amplitudes, integrals, hole_integrals, tile_mask, occupied_energy, virtual_energy):
    swap = [(0, 1), (1, 0)]
    z = lax.axis_size("row")
    a = amplitudes

    def ring(value, d):
        return lax.ppermute(value, "row", [(i, (i + d) % z) for i in range(z)])

    first, own_far, second = pack("pack_first", tile_mask, integrals, [(*FAR, False), (*FAR, True), (*REST, False)])
    v1 = lax.ppermute(first, "layer", swap)
    ap = lax.ppermute(a, "layer", swap)
    high, low = [ring(a, 1)], [ring(a, -1)]
    v2 = lax.ppermute(second, "layer", swap)
    [own_v] = pack("pack_own", tile_mask, integrals, [(*REST, True)], [own_far])

    up, down = far(a, ap, own_far, v1)
    far_up, far_down = send(up, True, 1), send(down, True, -1)
    here = hand_on([high[0], low[0]], [up], LONG)
    high.append(ring(here[0], 1))
    low.append(ring(here[1], -1))
    up, down, up_st, down_st = near(a, ap, own_v, v2, here)
    near_down, near_up = send(up, True, 1), send(down, True, -1)
    up = relay(far_up, up_st)
    far_up = send(up, True, 1)
    down = relay(far_down, down_st, [up])
    far_down = send(down, True, -1)
    here = hand_on([high[1], low[1]], [down], LONG)
    high.append(ring(here[0], 1))
    low.append(ring(here[1], -1))
    st = home(a, ap, own_v, v2, near_up, near_down, here)
    here = hand_on([high[2]], [st])
    high.append(ring(here[0], 1))
    own, m1, m2, m3 = turn(st, far_up, far_down, here)
    got = send(m2, False, 2), send(m1, False, 1), send(m3, False, -1)
    low[2:] = hand_on(low[2:], [m1, m2, m3])
    blocks, away = [a, *high, *low], [0, -1, -2, -3, -4, 1, 2, 3]
    total, inverse = hole_part(hole_integrals, blocks, away, own, occupied_energy, virtual_energy, [m1, m2, m3])
    return finish(total, inverse, got)


def solution(mesh):
    return jax.shard_map(
        shards,
        mesh=mesh,
        in_specs=(
            P("row", ("col", "layer")),
            P(("col", "layer"), None),
            P("row", None),
            P(),
            P("row"),
            P(("col", "layer")),
        ),
        out_specs=P("row", ("col", "layer")),
        check_vma=False,
    )
```

```python
import jax
import jax.numpy as jnp
from jax import lax
from jax.experimental import pallas as pl
from jax.experimental.pallas import tpu as pltpu
from jax.sharding import PartitionSpec as P

TB = 128
X = 4
Y = 4
F32 = jnp.float32
I16 = jnp.int16
I32 = jnp.int32
BF16 = jnp.bfloat16
TOP = 32700.0
STEPS = 64.0
SCALE = 1000
VMEM = 10 * 1024 * 1024
SM = pl.BlockSpec(memory_space=pltpu.SMEM)
VM = pl.BlockSpec(memory_space=pltpu.VMEM)
ANY = pl.BlockSpec(memory_space=pl.ANY)

FAR, REST = (0, 4), (4, 12)


def hop(first, d):
    pairs = []
    for y in range(Y):
        for x in range(X):
            for layer in range(2):
                along_x = (layer == 0) == first
                to = (y * X + (x + d) % X) if along_x else ((y + d) % Y * X + x)
                pairs.append(((y * X + x) * 2 + layer, to * 2 + layer))
    return pairs


def send(value, first, d):
    return lax.ppermute(value, ("col", "layer"), hop(first, d))


def run(body, after, operands, in_specs, out_shape, out_specs, carry=(), **kw):
    n, m, c = len(operands), len(after), len(carry)
    single = not isinstance(out_shape, list)
    shapes, specs = ([out_shape], [out_specs]) if single else (out_shape, out_specs)
    k = len(shapes)

    def whole(*refs):
        ins, outs = refs[:n + c + m], refs[n + c + m:]
        for i in range(c):
            outs[k + i][...] = ins[n + i][...]
        body(*ins[:n], *outs[:k], *outs[k + c:])

    out = pl.pallas_call(
        whole,
        in_specs=list(in_specs) + [VM] * c + [ANY] * m,
        out_shape=list(shapes) + [pltpu.VMEM(v.shape, v.dtype) for v in carry],
        out_specs=list(specs) + [VM] * c,
        compiler_params=params(),
        **kw,
    )(*operands, *map(inside, carry), *after)
    return out[0] if single and not c else out


def inside(value):
    return pltpu.with_memory_space_constraint(value, pltpu.VMEM)


def params():
    return pltpu.CompilerParams(vmem_limit_bytes=VMEM)


def cost(flops, moved):
    return pl.CostEstimate(flops=int(flops) // SCALE, bytes_accessed=int(moved) // SCALE, transcendentals=0)


LONG = cost(2 * 10 ** 13, 0)


def loop(n, unroll=1):
    def run(step):
        lax.fori_loop(0, n, lambda i, c: (step(i), c)[1], 0, unroll=unroll)
    return run


def rows_at(i, n):
    return pl.ds(pl.multiple_of(i * n, n), n)


def encode(block):
    peak = jnp.maximum(jnp.max(jnp.abs(block), axis=0, keepdims=True), 1e-30)
    code = jnp.floor(jnp.log2(TOP / peak) * STEPS)
    scale = jnp.exp2(code * (1.0 / STEPS))
    return jnp.round(block * scale).astype(I32).astype(I16), code


def put(ref, k, block):
    coded, code = encode(block)
    ref[rows_at(k, TB), :] = coded
    last = slice(ref.shape[0] - 16, ref.shape[0])
    rows = ref[last, :].astype(I32)
    at = lax.broadcasted_iota(I32, rows.shape, 0) == k
    ref[last, :] = jnp.where(at, code.astype(I32), rows).astype(I16)


def get(ref, k):
    rows = ref[ref.shape[0] - 16:, :].astype(I32)
    at = lax.broadcasted_iota(I32, rows.shape, 0) == k
    code = jnp.sum(jnp.where(at, rows, 0).astype(F32), axis=0, keepdims=True)
    scale = jnp.exp2(code * (1.0 / STEPS))
    return ref[rows_at(k, TB), :].astype(I32).astype(F32) * (1.0 / scale)


def pack(name, mask, integrals, parts, after=()):
    width = integrals.shape[0]
    tiles = width // TB
    total = sum(n for _, n, _ in parts)

    def body(mask_ref, v_ref, *refs):
        outs, (mask_s, sem, mask_sem) = refs[len(after):-3], refs[-3:]
        mask_copy = pltpu.make_async_copy(mask_ref, mask_s, mask_sem)
        mask_copy.start()
        col, layer = lax.axis_index("col"), lax.axis_index("layer")
        x, y = lax.rem(col, X), lax.div(col, X)
        row = (col * 2 + layer) * tiles

        def source(place, mine):
            who = layer if mine else 1 - layer
            d, o = jnp.right_shift(place, 2), jnp.bitwise_and(place, 3)
            d = jnp.where(d == 0, 2, jnp.where(d == 1, 1, jnp.where(d == 2, 3, 0)))
            dx, dy = jnp.where(who == 0, d, o), jnp.where(who == 0, o, d)
            return (lax.rem(y + dy, Y) * X + lax.rem(x + dx, X)) * 2 + who

        def copy(out, k, at, slot):
            return pltpu.make_async_copy(
                v_ref.at[:, pl.ds(pl.multiple_of(at * width, width), width)], out.at[k], sem.at[slot]
            )

        slots = [sum(n for _, n, _ in parts[:p]) for p in range(len(parts))]
        for (start, n, mine), out, slot in zip(parts, outs, slots):
            @loop(n)
            def _(k):
                copy(out, k, source(start + k, mine), slot + k).start()
        mask_copy.wait()
        for (start, n, mine), out, slot in zip(parts, outs, slots):
            @loop(n)
            def _(k):
                at = source(start + k, mine)
                copy(out, k, at, slot + k).wait()
                for kt in range(tiles):
                    for qt in range(tiles):
                        here = (k, slice(kt * TB, (kt + 1) * TB), slice(qt * TB, (qt + 1) * TB))

                        @pl.when(mask_s[row + kt, at * tiles + qt] == 0)
                        def _():
                            out[here] = jnp.zeros((TB, TB), BF16)

    return pl.pallas_call(
        body,
        out_shape=[pltpu.VMEM((n, width, width), BF16) for _, n, _ in parts],
        in_specs=[ANY, ANY] + [ANY] * len(after),
        out_specs=[VM] * len(parts),
        scratch_shapes=[pltpu.SMEM(mask.shape, I32), pltpu.SemaphoreType.DMA((total,)), pltpu.SemaphoreType.DMA(())],
        compiler_params=params(),
        cost_estimate=cost(0, 4 * total * width * width),
        name=name,
    )(*(pltpu.with_memory_space_constraint(v, pltpu.HBM) for v in (mask, integrals)), *after)


def product(lhs, own_ref, k, their_ref, their_k):
    return jnp.dot(lhs, jnp.concatenate([own_ref[k], their_ref[their_k]], axis=0), preferred_element_type=F32)


def left(a_ref, ap_ref):
    return jnp.concatenate([a_ref[...], ap_ref[...]], axis=1)


def hand_on(blocks, after, estimate=cost(0, 0)):
    return run(lambda: None, after, [], [], [], [], blocks, cost_estimate=estimate, name="hand_on")


def far(a, ap, own_v, v1, after=(), carry=()):
    rows, width = a.shape
    half = rows // 2
    n = half // TB
    msg = 4 * half + 16

    def body(a_ref, ap_ref, own_ref, v1_ref, up_ref, down_ref):
        lhs = left(a_ref, ap_ref)

        @loop(4, 2)
        def _(o):
            part = product(lhs, own_ref, o, v1_ref, o)
            for b in range(n):
                put(up_ref, o * n + b, part[b * TB:(b + 1) * TB])
                put(down_ref, o * n + b, part[half + b * TB:half + (b + 1) * TB])

    return run(
        body,
        after,
        [*map(inside, (a, ap, own_v, v1))],
        [VM] * 4,
        out_shape=[pltpu.VMEM((msg, width), I16)] * 2,
        out_specs=[VM] * 2,
        cost_estimate=cost(2 * 4 * rows * 2 * width * width, 4 * 4 * width * width),
        carry=carry,
        name="far",
    )


def near(a, ap, own_v, v2, after=(), carry=()):
    rows, width = a.shape
    half = rows // 2
    n = half // TB
    msg = 4 * half + 16

    def body(a_ref, ap_ref, own_ref, v2_ref, up_ref, down_ref, up_st, down_st):
        lhs = left(a_ref, ap_ref)

        @loop(4, 2)
        def _(o):
            part = product(lhs, own_ref, o, v2_ref, o)
            up_st[rows_at(o, half), :] = part[:half]
            for b in range(n):
                put(up_ref, o * n + b, part[half + b * TB:half + (b + 1) * TB])
            part = product(lhs, own_ref, 4 + o, v2_ref, 4 + o)
            down_st[rows_at(o, half), :] = part[half:]
            for b in range(n):
                put(down_ref, o * n + b, part[b * TB:(b + 1) * TB])

    return run(
        body,
        after,
        [*map(inside, (a, ap, own_v, v2))],
        [VM] * 4,
        out_shape=[pltpu.VMEM((msg, width), I16)] * 2 + [pltpu.VMEM((4 * half, width), F32)] * 2,
        out_specs=[VM] * 4,
        cost_estimate=LONG,
        carry=carry,
        name="near",
    )


def home(a, ap, own_v, v2, near_up, near_down, after=(), carry=()):
    rows, width = a.shape
    n = rows // TB
    h = n // 2

    def body(a_ref, ap_ref, own_ref, v2_ref, up_ref, down_ref, out_ref):
        lhs = left(a_ref, ap_ref)

        @loop(4, 2)
        def _(o):
            part = product(lhs, own_ref, 8 + o, v2_ref, 8 + o)
            for b in range(n):
                here = slice(b * TB, (b + 1) * TB)
                out_ref[o, here, :] = part[here] + get(up_ref if b < h else down_ref, o * h + b % h)

    return run(
        body,
        after,
        [*map(inside, (a, ap, own_v, v2, near_up, near_down))],
        [VM] * 6,
        out_shape=pltpu.VMEM((4, rows, width), F32),
        out_specs=VM,
        cost_estimate=LONG,
        carry=carry,
        name="home",
    )


def relay(got, own, after=(), carry=()):
    rows, width = own.shape

    def body(got_ref, own_ref, out_ref):
        @loop(rows // TB)
        def _(k):
            put(out_ref, k, own_ref[rows_at(k, TB), :] + get(got_ref, k))

    return run(
        body,
        after,
        [*map(inside, (got, own))],
        [VM] * 2,
        out_shape=pltpu.VMEM(got.shape, I16),
        out_specs=VM,
        cost_estimate=cost(0, 8 * rows * width),
        carry=carry,
        name="relay",
    )


def turn(st, far_up, far_down, after=(), carry=()):
    _, rows, width = st.shape
    n = rows // TB
    h = n // 2

    def body(st_ref, up_ref, down_ref, own_ref, m1_ref, m2_ref, m3_ref):
        for o, ref in ((2, m2_ref), (1, m1_ref), (3, m3_ref), (0, own_ref)):
            for b in range(n):
                part = st_ref[o, b * TB:(b + 1) * TB, :] + get(up_ref if b < h else down_ref, o * h + b % h)
                if o == 0:
                    ref[b * TB:(b + 1) * TB, :] = part
                else:
                    put(ref, b, part)

    return run(
        body,
        after,
        [*map(inside, (st, far_up, far_down))],
        [VM] * 3,
        out_shape=[pltpu.VMEM((rows, width), F32)] + [pltpu.VMEM((rows + 16, width), I16)] * 3,
        out_specs=[VM] * 4,
        cost_estimate=cost(0, 4 * rows * width * 10),
        carry=carry,
        name="turn",
    )


def hole_part(hole_integrals, blocks, away, own, occupied, virtual, after=()):
    rows = hole_integrals.shape[0]
    depth, width = blocks[0].shape
    count = hole_integrals.shape[1] // depth

    def body(h_ref, own_ref, occ_ref, virt_ref, *refs):
        sum_ref, inverse_ref = refs[-2:]
        here = lax.axis_index("row")
        virt = virt_ref[...]
        for b in range(rows // TB):
            at = slice(b * TB, (b + 1) * TB)
            occ = jnp.broadcast_to(occ_ref[:, at], (TB, TB)).T
            inverse_ref[at, :] = 1.0 / (virt - jnp.concatenate([occ] * (width // TB), axis=1))
        total = own_ref[...]
        for ref, k in zip(refs, away):
            at = lax.rem(here + (k + count), count)
            total = total + jnp.dot(h_ref[:, rows_at(at, depth)], ref[...], preferred_element_type=F32)
        sum_ref[...] = total

    return run(
        body,
        after,
        [*map(inside, (hole_integrals, own)), occupied[None, :], virtual[None, :], *map(inside, blocks)],
        [VM] * (4 + len(blocks)),
        out_shape=[pltpu.VMEM((rows, width), F32)] * 2,
        out_specs=[VM] * 2,
        cost_estimate=LONG,
        name="holes",
    )


def finish(total, inverse, got):
    rows, width = total.shape
    n = rows // TB

    def body(sum_ref, inverse_ref, m1, m2, m3, out_hbm, out_ref, sem):
        copies = []
        for b in range(n):
            here = slice(b * TB, (b + 1) * TB)
            part = sum_ref[here, :] + get(m1, b) + get(m2, b) + get(m3, b)
            out_ref[here, :] = part * inverse_ref[here, :]
            copies.append(pltpu.make_async_copy(out_ref.at[here, :], out_hbm.at[here, :], sem.at[b]))
            copies[-1].start()
        for copy in copies:
            copy.wait()

    return pl.pallas_call(
        body,
        out_shape=jax.ShapeDtypeStruct((rows, width), F32),
        in_specs=[VM] * 5,
        out_specs=ANY,
        scratch_shapes=[pltpu.VMEM((rows, width), F32), pltpu.SemaphoreType.DMA((n,))],
        compiler_params=params(),
        cost_estimate=cost(0, 4 * rows * width * 6),
        name="finish",
    )(*map(inside, (total, inverse, *got)))


def shards(amplitudes, integrals, hole_integrals, tile_mask, occupied_energy, virtual_energy):
    swap = [(0, 1), (1, 0)]
    z = lax.axis_size("row")
    a = amplitudes

    def ring(value, d):
        return lax.ppermute(value, "row", [(i, (i + d) % z) for i in range(z)])

    first, own_far, second = pack("pack_first", tile_mask, integrals, [(*FAR, False), (*FAR, True), (*REST, False)])
    v1 = lax.ppermute(first, "layer", swap)
    ap = lax.ppermute(a, "layer", swap)
    high, low = [ring(a, 1)], [ring(a, -1)]
    v2 = lax.ppermute(second, "layer", swap)
    [own_v] = pack("pack_own", tile_mask, integrals, [(*REST, True)], [own_far])

    up, down = far(a, ap, own_far, v1)
    far_up, far_down = send(up, True, 1), send(down, True, -1)
    here = hand_on([high[0], low[0]], [up], LONG)
    high.append(ring(here[0], 1))
    low.append(ring(here[1], -1))
    up, down, up_st, down_st = near(a, ap, own_v, v2, here)
    near_down, near_up = send(up, True, 1), send(down, True, -1)
    up = relay(far_up, up_st)
    far_up = send(up, True, 1)
    down = relay(far_down, down_st, [up])
    far_down = send(down, True, -1)
    here = hand_on([high[1], low[1]], [down], LONG)
    high.append(ring(here[0], 1))
    low.append(ring(here[1], -1))
    st = home(a, ap, own_v, v2, near_up, near_down, here)
    here = hand_on([high[2]], [st])
    high.append(ring(here[0], 1))
    own, m1, m2, m3 = turn(st, far_up, far_down, here)
    got = send(m2, False, 2), send(m1, False, 1), send(m3, False, -1)
    low[2:] = hand_on(low[2:], [m1, m2, m3])
    blocks, away = [a, *high, *low], [0, -1, -2, -3, -4, 1, 2, 3]
    total, inverse = hole_part(hole_integrals, blocks, away, own, occupied_energy, virtual_energy, [m1, m2, m3])
    return finish(total, inverse, got)


def solution(mesh):
    return jax.shard_map(
        shards,
        mesh=mesh,
        in_specs=(
            P("row", ("col", "layer")),
            P(("col", "layer"), None),
            P("row", None),
            P(),
            P("row"),
            P(("col", "layer")),
        ),
        out_specs=P("row", ("col", "layer")),
        check_vma=False,
    )
```
